32 devices in a mesh: dp: 8 (over z, x), tensor: 4 (over y, core).
Axes of the slice: x: 2, y: 2, z: 4, core: 2. Of those that a mesh axis runs over, the one named last changes fastest.
Arguments:
- hidden: float32 [8192, 640], P('dp'), may hold values from -6 to 6
- seq_lengths: int32 [8, 4], P('dp'), may hold values from 0 to 1024, as said below
- input_scale: float32 [640], replicated, may hold values from 0.25 to 1.75
- w_query: float32 [640, 1024], P(None, 'tensor'), may hold values from -0.25 to 0.25
- w_key: float32 [640, 256], replicated, may hold values from -0.25 to 0.25
- w_value: float32 [640, 256], replicated, may hold values from -0.25 to 0.25
- query_scale: float32 [256], replicated, may hold values from 0.25 to 1.75
- key_scale: float32 [256], replicated, may hold values from 0.25 to 1.75
- w_out: float32 [1024, 640], P('tensor'), may hold values from -0.1875 to 0.1875
- post_attn_scale: float32 [640], replicated, may hold values from 0.25 to 1.75
- pre_ffn_scale: float32 [640], replicated, may hold values from 0.25 to 1.75
- w_gate: float32 [640, 2048], P(None, 'tensor'), may hold values from -0.25 to 0.25
- w_up: float32 [640, 2048], P(None, 'tensor'), may hold values from -0.25 to 0.25
- w_down: float32 [2048, 640], P('tensor'), may hold values from -0.125 to 0.125
- post_ffn_scale: float32 [640], replicated, may hold values from 0.25 to 1.75
- out_cotangent: float32 [8192, 640], P('dp'), may hold values from -6 to 6
Outputs:
- output: float32 [8192, 640], P('dp')
- hidden_grad: float32 [8192, 640], P('dp')
- input_scale_grad: float32 [640], replicated
- w_query_grad: float32 [640, 1024], P(None, 'tensor')
- w_key_grad: float32 [640, 256], replicated
- w_value_grad: float32 [640, 256], replicated
- query_scale_grad: float32 [256], replicated
- key_scale_grad: float32 [256], replicated
- w_out_grad: float32 [1024, 640], P('tensor')
- post_attn_scale_grad: float32 [640], replicated
- pre_ffn_scale_grad: float32 [640], replicated
- w_gate_grad: float32 [640, 2048], P(None, 'tensor')
- w_up_grad: float32 [640, 2048], P(None, 'tensor')
- w_down_grad: float32 [2048, 640], P('tensor')
- post_ffn_scale_grad: float32 [640], replicated
The draws below stay inside these ranges and needn't reach their ends.
Inputs may be any that keep to these rules, and one draw needn't show every extreme that they name: `seq_lengths`: row d lists the lengths of the sequences held by index d of dp, in slot order, zeros for unused sequence slots; a row sums to at most 1024. In every draw exactly one row is a single sequence of 1024 tokens followed by zeros; every other row sums to between 128 and 896.
All inputs are finite; a program needn't handle non-finite values.
Results may differ from the reference program's by a relative error of at most 0.0003.
Values sent between devices are 32-bit elements; how exact they have to be, the bound alone decides.
A program may use at most 128 MiB of HBM per device.

```python
from functools import partial
import jax
import jax.numpy as jnp
from jax import lax

D = 640
HEADS = 4
HEAD_DIM = 256
FF = 2048
WINDOW = 512
CAP = 1024
SEQ_DEV = 4
ROWS = 8192
N_DP = 8


def draw_seq_lengths(key, part):
    first_key, second_key, third_key = jax.random.split(key, 3)
    device_loads = jax.random.randint(first_key, (N_DP,), CAP // 8, 7 * CAP // 8 + 1)
    heavy_device = jax.random.randint(second_key, (), 0, N_DP)
    cut_points = jax.random.randint(third_key, (N_DP, SEQ_DEV - 1), 0, device_loads[:, None] + 1)
    cut_points = jnp.sort(cut_points, axis=1)
    bounds = jnp.concatenate([jnp.zeros((N_DP, 1), jnp.int32), cut_points.astype(jnp.int32), device_loads[:, None].astype(jnp.int32)], axis=1)
    lengths = bounds[:, 1:] - bounds[:, :-1]
    single = jnp.zeros((SEQ_DEV,), jnp.int32).at[0].set(CAP)
    chosen = jnp.arange(N_DP)[:, None] == heavy_device
    return jnp.where(chosen, single[None, :], lengths).astype(jnp.int32)


def block_levels(rng, extent, cuts, least, high):
    level = 1.0
    for dim, shards_of in cuts:
        heights = jax.random.uniform(jax.random.fold_in(jax.random.fold_in(rng, 6), dim), (shards_of,), jnp.float32, least / len(cuts), high / len(cuts))
        level = level * jnp.repeat(jnp.exp(heights), extent[dim] // shards_of).reshape((-1,) + (1,) * (len(extent) - 1 - dim))
    return level


def scatter_about(stream_key, dims, width, most, cuts=(), kind=jnp.bfloat16):
    drawn = jax.random.normal(stream_key, dims, jnp.float32) * width
    if len(cuts) > 0:
        drawn = block_levels(stream_key, dims, cuts, -0.22, 0.18) * drawn
    return jnp.clip(drawn, min=-most, max=most).astype(kind)


def setup_inputs(seed: int = 0) -> dict:
    splits = jax.random.split(jax.random.key(seed), 17)
    hidden = scatter_about(splits[0], (ROWS, D), 1.0, 6.0, ((0, 8),), jnp.float32)
    seq_lengths = draw_seq_lengths(jax.random.fold_in(splits[16], 71), 0)
    input_scale = jnp.clip(1.0 + 0.15 * jax.random.normal(splits[2], (D,), jnp.float32), 0.25, 1.75)
    w_query = scatter_about(splits[3], (D, HEADS * HEAD_DIM), D ** -0.5, 0.25, ((1, 4),), jnp.float32)
    w_key = scatter_about(splits[4], (D, HEAD_DIM), D ** -0.5, 0.25, (), jnp.float32)
    w_value = scatter_about(splits[5], (D, HEAD_DIM), D ** -0.5, 0.25, (), jnp.float32)
    query_scale = jnp.clip(1.0 + 0.15 * jax.random.normal(splits[6], (HEAD_DIM,), jnp.float32), 0.25, 1.75)
    key_scale = jnp.clip(1.0 + 0.15 * jax.random.normal(splits[7], (HEAD_DIM,), jnp.float32), 0.25, 1.75)
    w_out = scatter_about(splits[8], (HEADS * HEAD_DIM, D), (HEADS * HEAD_DIM) ** -0.5, 0.1875, ((0, 4),), jnp.float32)
    post_attn_scale = jnp.clip(1.0 + 0.15 * jax.random.normal(splits[9], (D,), jnp.float32), 0.25, 1.75)
    pre_ffn_scale = jnp.clip(1.0 + 0.15 * jax.random.normal(splits[10], (D,), jnp.float32), 0.25, 1.75)
    w_gate = scatter_about(splits[11], (D, FF), D ** -0.5, 0.25, ((1, 4),), jnp.float32)
    w_up = scatter_about(splits[12], (D, FF), D ** -0.5, 0.25, ((1, 4),), jnp.float32)
    w_down = scatter_about(splits[13], (FF, D), FF ** -0.5, 0.125, ((0, 4),), jnp.float32)
    post_ffn_scale = jnp.clip(1.0 + 0.15 * jax.random.normal(splits[14], (D,), jnp.float32), 0.25, 1.75)
    out_cotangent = scatter_about(splits[15], (ROWS, D), 1.0, 6.0, ((0, 8),), jnp.float32)
    return dict(hidden=hidden, seq_lengths=seq_lengths, input_scale=input_scale, w_query=w_query, w_key=w_key, w_value=w_value, query_scale=query_scale, key_scale=key_scale, w_out=w_out, post_attn_scale=post_attn_scale, pre_ffn_scale=pre_ffn_scale, w_gate=w_gate, w_up=w_up, w_down=w_down, post_ffn_scale=post_ffn_scale, out_cotangent=out_cotangent)


epsilon = 1e-06
highest = lax.Precision.HIGHEST

@jax.custom_vjp
def low(v):
    return lax.optimization_barrier(v.astype(jnp.bfloat16)).astype(jnp.float32)

@jax.custom_vjp
def low_back(v):
    return v

def low_keep(v):
    return (low(v), None)

def low_pass(kept, grad):
    return (grad,)

def back_keep(v):
    return (v, None)

def back_low(kept, grad):
    return (low(grad),)
low.defvjp(low_keep, low_pass)
low_back.defvjp(back_keep, back_low)

def root_scale(values, gain):
    return values * lax.rsqrt(lax.optimization_barrier(jnp.mean(values * values, axis=-1, keepdims=True)) + epsilon) * gain

def rotate(values, cosine, sine):
    half_dim = values.shape[-1] // 2
    first_half = values[..., :half_dim]
    second_half = values[..., half_dim:]
    return jnp.concatenate([first_half * cosine - second_half * sine, second_half * cosine + first_half * sine], axis=-1)

def layout(lengths, row_count):
    bounds = jnp.concatenate([jnp.zeros((1,), jnp.int32), jnp.cumsum(lengths).astype(jnp.int32)])
    slot_index = jnp.arange(row_count, dtype=jnp.int32)
    segment = lax.optimization_barrier(jnp.sum((slot_index[:, None] >= bounds[None, 1:]).astype(jnp.int32), axis=1))
    starts = lax.optimization_barrier(jnp.max(jnp.where(bounds[None, :] <= slot_index[:, None], bounds[None, :], 0), axis=1))
    return (segment, slot_index - starts, slot_index < bounds[-1], slot_index)

def tables(positions, head_dim):
    half_dim = head_dim // 2
    frequency = 10000.0 ** (-2.0 * jnp.arange(half_dim).astype(jnp.float32) / head_dim)
    angles = positions.astype(jnp.float32)[:, None] * frequency[None, :]
    return (jnp.cos(angles), jnp.sin(angles))

def project_rows(inputs, gain, query_w, key_w, value_w, query_gain, key_gain, cosine, sine):
    normed = root_scale(inputs, gain)
    row_count = inputs.shape[0]
    queries = jnp.dot(normed, query_w, precision=highest).reshape(row_count, -1, key_w.shape[1])
    key_rows = jnp.dot(normed, key_w, precision=highest)
    value_rows = jnp.dot(normed, value_w, precision=highest)
    queries = rotate(root_scale(queries, query_gain), cosine[:, None, :], sine[:, None, :])
    key_rows = rotate(root_scale(key_rows, key_gain), cosine, sine)
    return (queries, key_rows, value_rows)

def middle(residual, branch, branch_gain, next_gain):
    hid_rows = residual + root_scale(branch, branch_gain)
    return (hid_rows, root_scale(hid_rows, next_gain))

def feed(inputs, gate_w, up_w, down_w):
    gated = jax.nn.gelu(jnp.dot(inputs, gate_w, precision=highest), approximate=True) * jnp.dot(inputs, up_w, precision=highest)
    return jnp.dot(gated, down_w, precision=highest)

def finish(branch, gain, residual):
    return residual + root_scale(branch, gain)

def attend_buffer(packed):
    queries, key_rows, value_rows, segment, slot_index = packed
    scores = jnp.einsum('ihd,jd->hij', queries, key_rows, precision=highest) * HEAD_DIM ** (-0.5)
    distance = slot_index[:, None] - slot_index[None, :]
    allowed = (segment[:, None] == segment[None, :]) & (distance >= 0) & (distance < WINDOW)
    scores = jnp.where(allowed[None], scores, -1e+30)
    weights = jax.nn.softmax(scores, axis=-1)
    return jnp.einsum('hij,jd->ihd', weights, value_rows, precision=highest)

def forward(hidden, input_scale, w_query, w_key, w_value, query_scale, key_scale, w_out, post_attn_scale, pre_ffn_scale, w_gate, w_up, w_down, post_ffn_scale, segment, slot_index, cosine, sine, live_rows):
    row_count = hidden.shape[0]
    queries, key_rows, value_rows = project_rows(hidden, input_scale, w_query, w_key, w_value, query_scale, key_scale, cosine, sine)
    buffer_count = row_count // CAP
    mixed = lax.map(jax.checkpoint(attend_buffer), (queries.reshape(buffer_count, CAP, HEADS, HEAD_DIM), key_rows.reshape(buffer_count, CAP, HEAD_DIM), value_rows.reshape(buffer_count, CAP, HEAD_DIM), segment.reshape(buffer_count, CAP), slot_index.reshape(buffer_count, CAP)))
    mixed = mixed.reshape(row_count, HEADS * HEAD_DIM)
    attn = jnp.dot(mixed, w_out, precision=highest)
    hid_rows, ffn_in = middle(hidden, attn, post_attn_scale, pre_ffn_scale)
    mlp = feed(ffn_in, w_gate, w_up, w_down)
    return finish(mlp, post_ffn_scale, hid_rows) * live_rows

def reference(hidden, seq_lengths, input_scale, w_query, w_key, w_value, query_scale, key_scale, w_out, post_attn_scale, pre_ffn_scale, w_gate, w_up, w_down, post_ffn_scale, out_cotangent):
    segment, positions, live_mask, slot_index = jax.vmap(partial(layout, row_count=CAP))(seq_lengths)
    segment = segment.reshape(-1)
    positions = positions.reshape(-1)
    slot_index = slot_index.reshape(-1)
    live_rows = live_mask.reshape(-1).astype(jnp.float32)[:, None]
    cosine, sine = tables(positions, HEAD_DIM)
    bound_forward = partial(forward, segment=segment, slot_index=slot_index, cosine=cosine, sine=sine, live_rows=live_rows)
    output, pullback = jax.vjp(bound_forward, hidden, input_scale, w_query, w_key, w_value, query_scale, key_scale, w_out, post_attn_scale, pre_ffn_scale, w_gate, w_up, w_down, post_ffn_scale)
    grads = pullback(out_cotangent)
    return (output, grads[0], grads[1], grads[2], grads[3], grads[4], grads[5], grads[6], grads[7], grads[8], grads[9], grads[10], grads[11], grads[12], grads[13])
```

```python
from functools import partial

import jax
import jax.numpy as jnp
from jax import lax
from jax.experimental import pallas as pl
from jax.experimental.pallas import tpu as pltpu
from jax.sharding import PartitionSpec as P

WINDOW = 512


epsilon = 1e-06
highest = lax.Precision.HIGH


def root_scale(values, gain):
    return values * lax.rsqrt(jnp.mean(values * values, axis=-1, keepdims=True) + epsilon) * gain


def rotate(values, cosine, sine):
    half_dim = values.shape[-1] // 2
    first_half = values[..., :half_dim]
    second_half = values[..., half_dim:]
    return jnp.concatenate(
        [first_half * cosine - second_half * sine, second_half * cosine + first_half * sine],
        axis=-1,
    )


def layout(lengths, row_count):
    count = lengths.shape[0]
    before = jnp.arange(count)[:, None] < jnp.arange(count + 1)[None, :]
    bounds = jnp.sum(jnp.where(before, lengths[:, None], 0), axis=0)
    slot_index = jnp.arange(row_count, dtype=jnp.int32)
    segment = jnp.sum((slot_index[:, None] >= bounds[None, 1:]).astype(jnp.int32), axis=1)
    starts = jnp.max(jnp.where(bounds[None, :] <= slot_index[:, None], bounds[None, :], 0), axis=1)
    return (segment, slot_index - starts, slot_index < bounds[-1], slot_index)


def tables(positions, head_dim):
    half_dim = head_dim // 2
    frequency = 10000.0 ** (-2.0 * jnp.arange(half_dim).astype(jnp.float32) / head_dim)
    angles = positions.astype(jnp.float32)[:, None] * frequency[None, :]
    return (jnp.cos(angles), jnp.sin(angles))


def middle(residual, branch, branch_gain, next_gain):
    hid_rows = residual + root_scale(branch, branch_gain)
    return (hid_rows, root_scale(hid_rows, next_gain))


def feed(inputs, gate_w, up_w, down_w):
    gated = jax.nn.gelu(jnp.dot(inputs, gate_w, precision=highest), approximate=True) * jnp.dot(
        inputs, up_w, precision=highest
    )
    return jnp.dot(gated, down_w, precision=highest)


def finish(branch, gain, residual):
    return residual + root_scale(branch, gain)


def share_kernel(chunks, x_ref, out_ref, near, total, far, sems):
    me = lax.axis_index("tensor")
    side = lax.rem(me, 2)
    near_dev = me + 1 - 2 * side
    far_dev = lax.rem(me + 2, 4)
    barrier = pltpu.get_barrier_semaphore()
    for partner in (near_dev, far_dev):
        pl.semaphore_signal(
            barrier, inc=1, device_id={"tensor": partner}, device_id_type=pl.DeviceIdType.MESH
        )
    pl.semaphore_wait(barrier, 2)
    half = x_ref.shape[0] // 2
    size = half // chunks

    def rows(first, c):
        return pl.ds(pl.multiple_of(first * half + c * size, 8), size)

    def send(stage, c, source, target, device):
        copy = pltpu.make_async_remote_copy(
            src_ref=source,
            dst_ref=target,
            send_sem=sems.at[stage, 0, c],
            recv_sem=sems.at[stage, 1, c],
            device_id={"tensor": device},
            device_id_type=pl.DeviceIdType.MESH,
        )
        copy.start()
        return copy

    first = [
        send(0, c, x_ref.at[rows(1 - side, c)], near.at[pl.ds(c * size, size)], near_dev)
        for c in range(chunks)
    ]
    second = []
    for c in range(chunks):
        here = pl.ds(c * size, size)
        first[c].wait_recv()
        total[here] = x_ref[rows(side, c)] + near[here]
        second.append(send(1, c, total.at[here], far.at[here], far_dev))
    third = []
    for c in range(chunks):
        here = pl.ds(c * size, size)
        second[c].wait_recv()
        out_ref[rows(side, c)] = total[here] + far[here]
        third.append(send(2, c, out_ref.at[rows(side, c)], out_ref.at[rows(side, c)], near_dev))
    for c in range(chunks):
        third[c].wait_recv()
    for copy in first + second + third:
        copy.wait_send()


def share(x, collective_id, chunks):
    if lax.axis_size("tensor") != 4:
        return lax.psum(x, "tensor")
    row_count, width = x.shape
    half = (row_count // 2, width)
    return pl.pallas_call(
        partial(share_kernel, chunks),
        out_shape=jax.ShapeDtypeStruct(x.shape, jnp.float32),
        in_specs=[pl.BlockSpec(memory_space=pltpu.VMEM)],
        out_specs=pl.BlockSpec(memory_space=pltpu.VMEM),
        scratch_shapes=[
            pltpu.VMEM(half, jnp.float32),
            pltpu.VMEM(half, jnp.float32),
            pltpu.VMEM(half, jnp.float32),
            pltpu.SemaphoreType.DMA((3, 2, chunks)),
        ],
        compiler_params=pltpu.CompilerParams(
            collective_id=collective_id, has_side_effects=True, vmem_limit_bytes=32 * 2**20
        ),
        cost_estimate=pl.CostEstimate(
            flops=x.size * 2, bytes_accessed=x.size * 8, transcendentals=0
        ),
    )(x)


def heads(projected, query_gain, key_gain, cosine, sine):
    head_dim = key_gain.shape[0]
    value_cols = projected.shape[1] - head_dim
    key_cols = value_cols - head_dim
    row_count = projected.shape[0]
    queries = projected[:, :key_cols].reshape(row_count, -1, head_dim)
    queries = rotate(root_scale(queries, query_gain), cosine[:, None, :], sine[:, None, :])
    key_rows = rotate(root_scale(projected[:, key_cols:value_cols], key_gain), cosine, sine)
    return (queries, key_rows, projected[:, value_cols:])


def dot(a, b, dims):
    return lax.dot_general(
        a, b, (dims, ((), ())), precision=highest, preferred_element_type=jnp.float32
    )


rows_rows = ((0,), (0,))
plain = ((1,), (0,))
cols_cols = ((1,), (1,))


def on_device(
    hidden,
    seq_lengths,
    input_scale,
    w_query,
    w_key,
    w_value,
    query_scale,
    key_scale,
    w_out,
    post_attn_scale,
    pre_ffn_scale,
    w_gate,
    w_up,
    w_down,
    post_ffn_scale,
    out_cotangent,
):
    row_count, width = hidden.shape
    head_dim = w_key.shape[1]
    head_count = w_query.shape[1] // head_dim
    scale = head_dim ** (-0.5)
    segment, positions, live_mask, slot_index = layout(seq_lengths[0], row_count)
    cosine, sine = tables(positions, head_dim)
    live_rows = live_mask.astype(jnp.float32)[:, None]
    normed, input_back = jax.vjp(root_scale, hidden, input_scale)
    w_all = jnp.concatenate([w_query, w_key, w_value], axis=1)
    projected = dot(normed, w_all, plain)
    (queries, key_rows, value_rows), heads_back = jax.vjp(
        partial(heads, cosine=cosine, sine=sine), projected, query_scale, key_scale
    )
    block_rows = min(WINDOW, row_count)
    block_count = row_count // block_rows
    kept = []
    mixed_heads = [[] for _ in range(head_count)]
    for b in range(block_count):
        q_rows = slice(b * block_rows, (b + 1) * block_rows)
        k_rows = slice(max(b - 1, 0) * block_rows, (b + 1) * block_rows)
        distance = slot_index[q_rows, None] - slot_index[None, k_rows]
        allowed = (
            (segment[q_rows, None] == segment[None, k_rows])
            & (distance >= 0)
            & (distance < WINDOW)
        )
        for h in range(head_count):
            scores = dot(queries[q_rows, h], key_rows[k_rows], cols_cols) * scale
            scores = jnp.where(allowed, scores, -1e30)
            weights = jnp.exp(scores - jnp.max(scores, axis=-1, keepdims=True))
            weights = weights / jnp.sum(weights, axis=-1, keepdims=True)
            kept.append((q_rows, k_rows, h, weights))
            mixed_heads[h].append(dot(weights, value_rows[k_rows], plain))
    mixed = jnp.concatenate([jnp.concatenate(m, axis=0) for m in mixed_heads], axis=1)
    attn_whole = share(dot(mixed, w_out, plain), 0, 4)
    (hid_rows, ffn_in), middle_back = jax.vjp(
        middle, hidden, attn_whole, post_attn_scale, pre_ffn_scale
    )
    gate = dot(ffn_in, w_gate, plain)
    up = dot(ffn_in, w_up, plain)
    gated, gated_back = jax.vjp(lambda g, u: jax.nn.gelu(g, approximate=True) * u, gate, up)
    mlp_whole = share(dot(gated, w_down, plain), 0, 4)
    result, finish_back = jax.vjp(finish, mlp_whole, post_ffn_scale, hid_rows)
    output = result * live_rows
    out_grad = out_cotangent * live_rows
    mlp_grad, post_ffn_grad, hid_direct = finish_back(out_grad)
    gate_back, up_back = gated_back(dot(mlp_grad, w_down, cols_cols))
    down_grad = dot(gated, mlp_grad, rows_rows)
    gate_grad = dot(ffn_in, gate_back, rows_rows)
    up_grad = dot(ffn_in, up_back, rows_rows)
    ffn_in_part = dot(gate_back, w_gate, cols_cols) + dot(up_back, w_up, cols_cols)
    ffn_in_part, gate_grad, up_grad, down_grad = lax.optimization_barrier(
        (ffn_in_part, gate_grad, up_grad, down_grad)
    )
    early = lax.psum((gate_grad, up_grad, down_grad), "dp")
    ffn_in_grad = share(ffn_in_part, 0, 4)
    hidden_direct, attn_grad, post_attn_grad, pre_ffn_grad = middle_back((hid_direct, ffn_in_grad))
    mixed_grad = dot(attn_grad, w_out, cols_cols)
    out_weight_grad = dot(mixed, attn_grad, rows_rows)
    query_parts = [[] for _ in range(head_count)]
    key_blocks = [0.0] * block_count
    value_blocks = [0.0] * block_count
    for q_rows, k_rows, h, weights in kept:
        cols = slice(h * head_dim, (h + 1) * head_dim)
        grad_block = mixed_grad[q_rows, cols]
        row_dots = jnp.sum(grad_block * mixed[q_rows, cols], axis=-1, keepdims=True)
        value_part = dot(weights, grad_block, rows_rows)
        spread = dot(grad_block, value_rows[k_rows], cols_cols)
        score_grad = weights * (spread - row_dots) * scale
        query_parts[h].append(dot(score_grad, key_rows[k_rows], plain))
        key_part = dot(score_grad, queries[q_rows, h], rows_rows)
        for i in range((k_rows.stop - k_rows.start) // block_rows):
            b = k_rows.start // block_rows + i
            part = slice(i * block_rows, (i + 1) * block_rows)
            key_blocks[b] = key_blocks[b] + key_part[part]
            value_blocks[b] = value_blocks[b] + value_part[part]
    query_grad = jnp.stack([jnp.concatenate(q, axis=0) for q in query_parts], axis=1)
    projected_grad, query_gain_grad, key_gain_grad = heads_back(
        (query_grad, jnp.concatenate(key_blocks, axis=0), jnp.concatenate(value_blocks, axis=0))
    )
    normed_part = dot(projected_grad, w_all, cols_cols)
    w_all_grad = dot(projected_grad, normed, rows_rows)
    query_cols = head_count * head_dim
    shared = share(jnp.concatenate([normed_part, w_all_grad[query_cols:]], axis=0), 1, 6)
    hidden_attn, input_grad = input_back(shared[:row_count])
    hidden_grad = hidden_direct + hidden_attn
    tensor_size = lax.axis_size("tensor")
    me = lax.axis_index("tensor")
    quarter = 2 * head_dim // tensor_size
    kv_quarter = lax.dynamic_slice_in_dim(shared, row_count + me * quarter, quarter, 0)
    fill = jnp.zeros((width - 2 * head_dim,), jnp.float32)
    gains = jnp.stack(
        [
            jnp.concatenate([query_gain_grad, key_gain_grad, fill]),
            input_grad,
            post_attn_grad,
            pre_ffn_grad,
            post_ffn_grad,
        ]
        + [jnp.zeros((width,), jnp.float32)] * 3
    )
    late = jnp.concatenate([w_all_grad[:query_cols], kv_quarter, gains], axis=0)
    late, early = lax.optimization_barrier((late, early))
    late, out_weight_grad = lax.psum((late, out_weight_grad), "dp")
    gate_grad, up_grad, down_grad = early
    piece = quarter + 8
    spread_rows = lax.dynamic_update_slice_in_dim(
        jnp.zeros((tensor_size * piece, width), jnp.float32),
        late[query_cols : query_cols + piece],
        me * piece,
        0,
    )
    gathered = share(spread_rows, 2, 2).reshape(tensor_size, piece, width)
    kv_grad = gathered[:, :quarter].reshape(2 * head_dim, width)
    head_gains = jnp.sum(gathered[:, quarter], axis=0)
    gains = late[query_cols + quarter :]
    return (
        output,
        hidden_grad,
        gains[1],
        late[:query_cols].T,
        kv_grad[:head_dim].T,
        kv_grad[head_dim:].T,
        head_gains[:head_dim],
        head_gains[head_dim : 2 * head_dim],
        out_weight_grad,
        gains[2],
        gains[3],
        gate_grad,
        up_grad,
        down_grad,
        gains[4],
    )


def solution(mesh):
    placed = (
        P("dp", None),
        P("dp", None),
        P(),
        P(None, "tensor"),
        P(),
        P(),
        P(),
        P(),
        P("tensor", None),
        P(),
        P(),
        P(None, "tensor"),
        P(None, "tensor"),
        P("tensor", None),
        P(),
        P("dp", None),
    )
    return jax.shard_map(
        on_device,
        mesh=mesh,
        in_specs=placed,
        out_specs=(
            P("dp", None),
            P("dp", None),
            P(),
            P(None, "tensor"),
            P(),
            P(),
            P(),
            P(),
            P("tensor", None),
            P(),
            P(),
            P(None, "tensor"),
            P(None, "tensor"),
            P("tensor", None),
            P(),
        ),
        check_vma=False,
    )
```

```python
from functools import partial

import jax
import jax.numpy as jnp
from jax import lax
from jax.experimental import pallas as pl
from jax.experimental.pallas import tpu as pltpu
from jax.sharding import PartitionSpec as P

WINDOW = 512


epsilon = 1e-06
highest = lax.Precision.HIGH


def root_scale(values, gain):
    return values * lax.rsqrt(jnp.mean(values * values, axis=-1, keepdims=True) + epsilon) * gain


def rotate(values, cosine, sine):
    half_dim = values.shape[-1] // 2
    first_half = values[..., :half_dim]
    second_half = values[..., half_dim:]
    return jnp.concatenate(
        [first_half * cosine - second_half * sine, second_half * cosine + first_half * sine],
        axis=-1,
    )


def layout(lengths, row_count):
    count = lengths.shape[0]
    before = jnp.arange(count)[:, None] < jnp.arange(count + 1)[None, :]
    bounds = jnp.sum(jnp.where(before, lengths[:, None], 0), axis=0)
    slot_index = jnp.arange(row_count, dtype=jnp.int32)
    segment = jnp.sum((slot_index[:, None] >= bounds[None, 1:]).astype(jnp.int32), axis=1)
    starts = jnp.max(jnp.where(bounds[None, :] <= slot_index[:, None], bounds[None, :], 0), axis=1)
    return (segment, slot_index - starts, slot_index < bounds[-1], slot_index)


def tables(positions, head_dim):
    half_dim = head_dim // 2
    frequency = 10000.0 ** (-2.0 * jnp.arange(half_dim).astype(jnp.float32) / head_dim)
    angles = positions.astype(jnp.float32)[:, None] * frequency[None, :]
    return (jnp.cos(angles), jnp.sin(angles))


def middle(residual, branch, branch_gain, next_gain):
    hid_rows = residual + root_scale(branch, branch_gain)
    return (hid_rows, root_scale(hid_rows, next_gain))


def feed(inputs, gate_w, up_w, down_w):
    gated = jax.nn.gelu(jnp.dot(inputs, gate_w, precision=highest), approximate=True) * jnp.dot(
        inputs, up_w, precision=highest
    )
    return jnp.dot(gated, down_w, precision=highest)


def finish(branch, gain, residual):
    return residual + root_scale(branch, gain)


def share_kernel(chunks, x_ref, out_ref, near, total, far, sems):
    me = lax.axis_index("tensor")
    side = lax.rem(me, 2)
    near_dev = me + 1 - 2 * side
    far_dev = lax.rem(me + 2, 4)
    barrier = pltpu.get_barrier_semaphore()
    for partner in (near_dev, far_dev):
        pl.semaphore_signal(
            barrier, inc=1, device_id={"tensor": partner}, device_id_type=pl.DeviceIdType.MESH
        )
    pl.semaphore_wait(barrier, 2)
    half = x_ref.shape[0] // 2
    size = half // chunks

    def rows(first, c):
        return pl.ds(pl.multiple_of(first * half + c * size, 8), size)

    def send(stage, c, source, target, device):
        copy = pltpu.make_async_remote_copy(
            src_ref=source,
            dst_ref=target,
            send_sem=sems.at[stage, 0, c],
            recv_sem=sems.at[stage, 1, c],
            device_id={"tensor": device},
            device_id_type=pl.DeviceIdType.MESH,
        )
        copy.start()
        return copy

    first = [
        send(0, c, x_ref.at[rows(1 - side, c)], near.at[pl.ds(c * size, size)], near_dev)
        for c in range(chunks)
    ]
    second = []
    for c in range(chunks):
        here = pl.ds(c * size, size)
        first[c].wait_recv()
        total[here] = x_ref[rows(side, c)] + near[here]
        second.append(send(1, c, total.at[here], far.at[here], far_dev))
    third = []
    for c in range(chunks):
        here = pl.ds(c * size, size)
        second[c].wait_recv()
        out_ref[rows(side, c)] = total[here] + far[here]
        third.append(send(2, c, out_ref.at[rows(side, c)], out_ref.at[rows(side, c)], near_dev))
    for c in range(chunks):
        third[c].wait_recv()
    for copy in first + second + third:
        copy.wait_send()


def share(x, collective_id, chunks):
    if lax.axis_size("tensor") != 4:
        return lax.psum(x, "tensor")
    row_count, width = x.shape
    half = (row_count // 2, width)
    return pl.pallas_call(
        partial(share_kernel, chunks),
        out_shape=jax.ShapeDtypeStruct(x.shape, jnp.float32),
        in_specs=[pl.BlockSpec(memory_space=pltpu.VMEM)],
        out_specs=pl.BlockSpec(memory_space=pltpu.VMEM),
        scratch_shapes=[
            pltpu.VMEM(half, jnp.float32),
            pltpu.VMEM(half, jnp.float32),
            pltpu.VMEM(half, jnp.float32),
            pltpu.SemaphoreType.DMA((3, 2, chunks)),
        ],
        compiler_params=pltpu.CompilerParams(
            collective_id=collective_id, has_side_effects=True, vmem_limit_bytes=32 * 2**20
        ),
        cost_estimate=pl.CostEstimate(
            flops=x.size * 2, bytes_accessed=x.size * 8, transcendentals=0
        ),
    )(x)


def gather_kernel(x_ref, out_ref, sems):
    me = lax.axis_index("tensor")
    side = lax.rem(me, 2)
    near_dev = me + 1 - 2 * side
    far_dev = lax.rem(me + 2, 4)
    barrier = pltpu.get_barrier_semaphore()
    for partner in (near_dev, far_dev):
        pl.semaphore_signal(
            barrier, inc=1, device_id={"tensor": partner}, device_id_type=pl.DeviceIdType.MESH
        )
    pl.semaphore_wait(barrier, 2)

    def send(stage, source, slot, device):
        copy = pltpu.make_async_remote_copy(
            src_ref=source,
            dst_ref=out_ref.at[slot],
            send_sem=sems.at[stage, 0],
            recv_sem=sems.at[stage, 1],
            device_id={"tensor": device},
            device_id_type=pl.DeviceIdType.MESH,
        )
        copy.start()
        return copy

    across = send(0, x_ref, me, far_dev)
    beside = send(1, x_ref, me, near_dev)
    out_ref[me] = x_ref[...]
    across.wait_recv()
    onward = send(2, out_ref.at[far_dev], far_dev, near_dev)
    beside.wait_recv()
    onward.wait_recv()
    for copy in (across, beside, onward):
        copy.wait_send()


def gather(x, collective_id):
    if lax.axis_size("tensor") != 4:
        return lax.all_gather(x, "tensor")
    return pl.pallas_call(
        gather_kernel,
        out_shape=jax.ShapeDtypeStruct((4, *x.shape), jnp.float32),
        in_specs=[pl.BlockSpec(memory_space=pltpu.VMEM)],
        out_specs=pl.BlockSpec(memory_space=pltpu.VMEM),
        scratch_shapes=[pltpu.SemaphoreType.DMA((3, 2))],
        compiler_params=pltpu.CompilerParams(
            collective_id=collective_id, has_side_effects=True, vmem_limit_bytes=32 * 2**20
        ),
        cost_estimate=pl.CostEstimate(flops=0, bytes_accessed=x.size * 20, transcendentals=0),
    )(x)


def total_kernel(parts, x_ref, out_ref, total, landed, sems):
    me = lax.axis_index("dp")
    sides = [lax.rem(me // 2**bit, 2) for bit in range(3)]
    partners = [me + (1 - 2 * sides[bit]) * 2**bit for bit in range(3)]
    barrier = pltpu.get_barrier_semaphore()
    for partner in partners:
        pl.semaphore_signal(
            barrier, inc=1, device_id={"dp": partner}, device_id_type=pl.DeviceIdType.MESH
        )
    pl.semaphore_wait(barrier, 3)

    def span(first, size):
        return pl.ds(pl.multiple_of(first, 8), size)

    def send(stage, p, source, target, bit):
        copy = pltpu.make_async_remote_copy(
            src_ref=source,
            dst_ref=target,
            send_sem=sems.at[stage, 0, p],
            recv_sem=sems.at[stage, 1, p],
            device_id={"dp": partners[bit]},
            device_id_type=pl.DeviceIdType.MESH,
        )
        copy.start()
        copies.append(copy)
        return copy

    copies = []
    pending = [None] * len(parts)
    bases = [first for first, _, _ in parts]
    slots = [first for first, _, _ in parts]

    def halve(stage, p):
        first, size, order = parts[p]
        half = size // 2 ** (stage + 1)
        bit = order[stage]
        source = x_ref if stage == 0 else total
        give = bases[p] + (1 - sides[bit]) * half
        bases[p] = bases[p] + sides[bit] * half
        pending[p] = send(
            stage, p, source.at[span(give, half)], landed.at[pl.ds(slots[p], half)], bit
        )

    def double(stage, p):
        size = parts[p][1] // 2 ** (stage + 1)
        rows = out_ref.at[span(bases[p], size)]
        bit = parts[p][2][stage]
        pending[p] = send(5 - stage, p, rows, rows, bit)
        bases[p] = bases[p] - sides[bit] * size

    for p in range(len(parts)):
        halve(0, p)
    for stage in range(3):
        for p in range(len(parts)):
            half = parts[p][1] // 2 ** (stage + 1)
            pending[p].wait_recv()
            keep = span(bases[p], half)
            source = x_ref if stage == 0 else total
            target = out_ref if stage == 2 else total
            target[keep] = source[keep] + landed[pl.ds(slots[p], half)]
            slots[p] = slots[p] + half
            if stage < 2:
                halve(stage + 1, p)
            else:
                double(2, p)
    for stage in (1, 0):
        for p in range(len(parts)):
            pending[p].wait_recv()
            double(stage, p)
    for p in range(len(parts)):
        pending[p].wait_recv()
    for copy in copies:
        copy.wait_send()


def total_rows(x, collective_id):
    if lax.axis_size("dp") != 8:
        return lax.psum(x, "dp")
    row_count, width = x.shape
    units = -(-row_count // 64)
    x = jnp.pad(x, ((0, units * 64 - row_count), (0, 0)))
    cut = (units + 1) // 2 * 64
    parts = ((0, cut, (0, 1, 2)), (cut, x.shape[0] - cut, (1, 2, 0)))
    whole = pltpu.VMEM(x.shape, jnp.float32)
    return pl.pallas_call(
        partial(total_kernel, parts),
        out_shape=jax.ShapeDtypeStruct(x.shape, jnp.float32),
        in_specs=[pl.BlockSpec(memory_space=pltpu.VMEM)],
        out_specs=pl.BlockSpec(memory_space=pltpu.VMEM),
        scratch_shapes=[whole, whole, pltpu.SemaphoreType.DMA((6, 2, len(parts)))],
        compiler_params=pltpu.CompilerParams(
            collective_id=collective_id, has_side_effects=True, vmem_limit_bytes=32 * 2**20
        ),
        cost_estimate=pl.CostEstimate(
            flops=x.size * 2, bytes_accessed=x.size * 8, transcendentals=0
        ),
    )(x)


def heads(projected, query_gain, key_gain, cosine, sine):
    head_dim = key_gain.shape[0]
    value_cols = projected.shape[1] - head_dim
    key_cols = value_cols - head_dim
    row_count = projected.shape[0]
    queries = projected[:, :key_cols].reshape(row_count, -1, head_dim)
    queries = rotate(root_scale(queries, query_gain), cosine[:, None, :], sine[:, None, :])
    key_rows = rotate(root_scale(projected[:, key_cols:value_cols], key_gain), cosine, sine)
    return (queries, key_rows, projected[:, value_cols:])


def dot(a, b, dims):
    return lax.dot_general(
        a, b, (dims, ((), ())), precision=highest, preferred_element_type=jnp.float32
    )


rows_rows = ((0,), (0,))
plain = ((1,), (0,))
cols_cols = ((1,), (1,))


def on_device(
    hidden,
    seq_lengths,
    input_scale,
    w_query,
    w_key,
    w_value,
    query_scale,
    key_scale,
    w_out,
    post_attn_scale,
    pre_ffn_scale,
    w_gate,
    w_up,
    w_down,
    post_ffn_scale,
    out_cotangent,
):
    row_count, width = hidden.shape
    head_dim = w_key.shape[1]
    head_count = w_query.shape[1] // head_dim
    scale = head_dim ** (-0.5)
    segment, positions, live_mask, slot_index = layout(seq_lengths[0], row_count)
    cosine, sine = tables(positions, head_dim)
    live_rows = live_mask.astype(jnp.float32)[:, None]
    normed, input_back = jax.vjp(root_scale, hidden, input_scale)
    w_all = jnp.concatenate([w_query, w_key, w_value], axis=1)
    projected = dot(normed, w_all, plain)
    (queries, key_rows, value_rows), heads_back = jax.vjp(
        partial(heads, cosine=cosine, sine=sine), projected, query_scale, key_scale
    )
    block_rows = min(WINDOW, row_count)
    block_count = row_count // block_rows
    kept = []
    mixed_heads = [[] for _ in range(head_count)]
    for b in range(block_count):
        q_rows = slice(b * block_rows, (b + 1) * block_rows)
        k_rows = slice(max(b - 1, 0) * block_rows, (b + 1) * block_rows)
        distance = slot_index[q_rows, None] - slot_index[None, k_rows]
        allowed = (
            (segment[q_rows, None] == segment[None, k_rows])
            & (distance >= 0)
            & (distance < WINDOW)
        )
        for h in range(head_count):
            scores = dot(queries[q_rows, h], key_rows[k_rows], cols_cols) * scale
            scores = jnp.where(allowed, scores, -1e30)
            weights = jnp.exp(scores - jnp.max(scores, axis=-1, keepdims=True))
            weights = weights / jnp.sum(weights, axis=-1, keepdims=True)
            kept.append((q_rows, k_rows, h, weights))
            mixed_heads[h].append(dot(weights, value_rows[k_rows], plain))
    mixed = jnp.concatenate([jnp.concatenate(m, axis=0) for m in mixed_heads], axis=1)
    attn_whole = share(dot(mixed, w_out, plain), 0, 4)
    (hid_rows, ffn_in), middle_back = jax.vjp(
        middle, hidden, attn_whole, post_attn_scale, pre_ffn_scale
    )
    gate = dot(ffn_in, w_gate, plain)
    up = dot(ffn_in, w_up, plain)
    gated, gated_back = jax.vjp(lambda g, u: jax.nn.gelu(g, approximate=True) * u, gate, up)
    mlp_whole = share(dot(gated, w_down, plain), 0, 4)
    result, finish_back = jax.vjp(finish, mlp_whole, post_ffn_scale, hid_rows)
    output = result * live_rows
    out_grad = out_cotangent * live_rows
    mlp_grad, post_ffn_grad, hid_direct = finish_back(out_grad)
    gate_back, up_back = gated_back(dot(mlp_grad, w_down, cols_cols))
    down_grad = dot(gated, mlp_grad, rows_rows)
    gate_grad = dot(ffn_in, gate_back, rows_rows)
    up_grad = dot(ffn_in, up_back, rows_rows)
    ffn_in_part = dot(gate_back, w_gate, cols_cols) + dot(up_back, w_up, cols_cols)
    ffn_in_part, gate_grad, up_grad, down_grad = lax.optimization_barrier(
        (ffn_in_part, gate_grad, up_grad, down_grad)
    )
    early = lax.psum((gate_grad, up_grad, down_grad), "dp")
    ffn_in_grad = share(ffn_in_part, 0, 4)
    hidden_direct, attn_grad, post_attn_grad, pre_ffn_grad = middle_back((hid_direct, ffn_in_grad))
    mixed_grad = dot(attn_grad, w_out, cols_cols)
    out_weight_grad = dot(mixed, attn_grad, rows_rows)
    query_parts = [[] for _ in range(head_count)]
    key_blocks = [0.0] * block_count
    value_blocks = [0.0] * block_count
    for q_rows, k_rows, h, weights in kept:
        cols = slice(h * head_dim, (h + 1) * head_dim)
        grad_block = mixed_grad[q_rows, cols]
        row_dots = jnp.sum(grad_block * mixed[q_rows, cols], axis=-1, keepdims=True)
        value_part = dot(weights, grad_block, rows_rows)
        spread = dot(grad_block, value_rows[k_rows], cols_cols)
        score_grad = weights * (spread - row_dots) * scale
        query_parts[h].append(dot(score_grad, key_rows[k_rows], plain))
        key_part = dot(score_grad, queries[q_rows, h], rows_rows)
        for i in range((k_rows.stop - k_rows.start) // block_rows):
            b = k_rows.start // block_rows + i
            part = slice(i * block_rows, (i + 1) * block_rows)
            key_blocks[b] = key_blocks[b] + key_part[part]
            value_blocks[b] = value_blocks[b] + value_part[part]
    query_grad = jnp.stack([jnp.concatenate(q, axis=0) for q in query_parts], axis=1)
    projected_grad, query_gain_grad, key_gain_grad = heads_back(
        (query_grad, jnp.concatenate(key_blocks, axis=0), jnp.concatenate(value_blocks, axis=0))
    )
    normed_part = dot(projected_grad, w_all, cols_cols)
    w_all_grad = dot(projected_grad, normed, rows_rows)
    query_cols = head_count * head_dim
    shared = share(jnp.concatenate([normed_part, w_all_grad[query_cols:]], axis=0), 1, 6)
    hidden_attn, input_grad = input_back(shared[:row_count])
    hidden_grad = hidden_direct + hidden_attn
    tensor_size = lax.axis_size("tensor")
    me = lax.axis_index("tensor")
    quarter = 2 * head_dim // tensor_size
    kv_quarter = lax.dynamic_slice_in_dim(shared, row_count + me * quarter, quarter, 0)
    fill = jnp.zeros((width - 2 * head_dim,), jnp.float32)
    gains = jnp.stack(
        [
            jnp.concatenate([query_gain_grad, key_gain_grad, fill]),
            input_grad,
            post_attn_grad,
            pre_ffn_grad,
            post_ffn_grad,
        ]
        + [jnp.zeros((width,), jnp.float32)] * 3
    )
    late = total_rows(
        jnp.concatenate([w_all_grad[:query_cols], out_weight_grad, kv_quarter, gains], axis=0), 3
    )
    kv_first = query_cols + out_weight_grad.shape[0]
    out_weight_grad = late[query_cols:kv_first]
    gate_grad, up_grad, down_grad = early
    gathered = gather(late[kv_first : kv_first + quarter + 8], 2)
    kv_grad = gathered[:, :quarter].reshape(2 * head_dim, width)
    head_gains = jnp.sum(gathered[:, quarter], axis=0)
    gains = late[kv_first + quarter :]
    return (
        output,
        hidden_grad,
        gains[1],
        late[:query_cols].T,
        kv_grad[:head_dim].T,
        kv_grad[head_dim:].T,
        head_gains[:head_dim],
        head_gains[head_dim : 2 * head_dim],
        out_weight_grad,
        gains[2],
        gains[3],
        gate_grad,
        up_grad,
        down_grad,
        gains[4],
    )


def solution(mesh):
    placed = (
        P("dp", None),
        P("dp", None),
        P(),
        P(None, "tensor"),
        P(),
        P(),
        P(),
        P(),
        P("tensor", None),
        P(),
        P(),
        P(None, "tensor"),
        P(None, "tensor"),
        P("tensor", None),
        P(),
        P("dp", None),
    )
    return jax.shard_map(
        on_device,
        mesh=mesh,
        in_specs=placed,
        out_specs=(
            P("dp", None),
            P("dp", None),
            P(),
            P(None, "tensor"),
            P(),
            P(),
            P(),
            P(),
            P("tensor", None),
            P(),
            P(),
            P(None, "tensor"),
            P(None, "tensor"),
            P("tensor", None),
            P(),
        ),
        check_vma=False,
    )
```
